1024 devices in a mesh: expert: 32 (over z), dp: 32 (over y, x, core).
Axes of the slice: x: 4, y: 4, z: 32, core: 2. Of those that a mesh axis runs over, the one named last changes fastest.
Arguments:
- rows_in: bfloat16 [16384, 4096], P('expert', 'dp'), may hold values from -6 to 6
- out_grad: bfloat16 [16384, 4096], P('expert', 'dp'), may hold values from -6 to 6
- route_weight: float32 [16384], P('expert'), may hold values from 0.1 to 1
- live_rows: int32 [32], P('expert'), may hold values from 1 to 512, as said below
- expert_of_group: int32 [32], replicated, may hold values from 0 to 31, as said below
- gate_weight: bfloat16 [32, 1536, 4096], P(None, 'expert', 'dp'), may hold values from -0.09375 to 0.09375
- up_weight: bfloat16 [32, 1536, 4096], P(None, 'expert', 'dp'), may hold values from -0.09375 to 0.09375
- down_weight: bfloat16 [32, 1536, 4096], P(None, 'expert', 'dp'), may hold values from -0.15625 to 0.15625
Outputs:
- rows_grad: bfloat16 [16384, 4096], P('expert', 'dp')
- gate_grad: bfloat16 [32, 1536, 4096], P(None, 'expert', 'dp')
- up_grad: bfloat16 [32, 1536, 4096], P(None, 'expert', 'dp')
- down_grad: bfloat16 [32, 1536, 4096], P(None, 'expert', 'dp')
The draws below stay inside these ranges and needn't reach their ends.
Inputs may be any that keep to these rules, and one draw needn't show every extreme that they name: `live_rows`: rows at or past a group's count are padding; some group has all 512 slots live. `expert_of_group`: several groups may use the same expert.
All inputs are finite; a program needn't handle non-finite values.
Results may differ from the reference program's by a relative error of at most 0.03.
Values may be sent and summed in bfloat16 or wider, within the bound.
No kernel may reach another device: no remote copies, remote signals or barrier semaphores. Data moves between devices by JAX's collectives and lax.ppermute only.
A program may use at most 32 MiB of HBM per device.

```python
import jax
import jax.numpy as jnp
from jax import lax

D = 4096
FF = 1536
EXPERTS = 32
ROWS = 512
GROUPS = 32
RTOTAL = 16384
N_DP = 32


def draw_live_rows(key, part):
    key = jax.random.fold_in(key, 11)
    first_key, second_key = jax.random.split(key)
    counts = jax.random.randint(first_key, (GROUPS,), 1, ROWS + 1)
    chosen = jax.random.randint(second_key, (), 0, GROUPS)
    return counts.at[chosen].set(ROWS).astype(jnp.int32)


def draw_expert_of_group(key, part):
    key = jax.random.fold_in(key, 23)
    keys = jax.random.split(key, 5)
    picks = jax.random.randint(keys[0], (GROUPS,), 0, EXPERTS)
    popular = jax.random.randint(keys[1], (), 0, EXPERTS)
    crowded = jax.random.randint(keys[2], (GROUPS,), 0, 4) == 0
    picks = jnp.where(crowded, popular, picks)
    first_slot = jax.random.randint(keys[3], (), 0, GROUPS)
    second_slot = (first_slot + 1 + jax.random.randint(keys[4], (), 0, GROUPS - 1)) % GROUPS
    return picks.at[first_slot].set(EXPERTS - 1).at[second_slot].set(0).astype(jnp.int32)


def shard_levels(rng, shape, pieces, smallest, largest):
    loudness, own = 1.0, jax.random.fold_in(rng, 6)
    for dim, parts in pieces:
        heights = jnp.exp(jax.random.uniform(jax.random.fold_in(own, dim), (parts,), jnp.float32, smallest / len(pieces), largest / len(pieces)))
        loudness = loudness * jnp.repeat(heights, shape[dim] // parts).reshape([-1 if axis == dim else 1 for axis in range(len(shape))])
    return loudness


def centred(stream_key, shape, scale, reach, shards=(), kind=jnp.bfloat16):
    result = scale * jax.random.normal(stream_key, shape, jnp.float32)
    if shards:
        result = result * shard_levels(stream_key, shape, shards, -0.22, 0.18)
    return jnp.clip(result, -reach, reach).astype(kind)


def setup_inputs(seed: int = 0) -> dict:
    arg_keys = jax.random.split(jax.random.key(seed), 9)
    rows_in = centred(arg_keys[0], (RTOTAL, D), 1.0, 6.0, ((0, 32), (1, 32)))
    out_grad = centred(arg_keys[1], (RTOTAL, D), 1.0, 6.0, ((0, 32), (1, 32)))
    route_weight = jnp.clip(0.1 + 0.9 * jax.random.uniform(arg_keys[2], (RTOTAL,), jnp.float32) ** shard_levels(arg_keys[2], (RTOTAL,), ((0, 32),), -0.2, 0.2), 0.1, 1.0)
    live_rows = draw_live_rows(jax.random.fold_in(arg_keys[8], 71), 0)
    expert_of_group = draw_expert_of_group(jax.random.fold_in(arg_keys[8], 71), 0)
    gate_weight = centred(arg_keys[5], (EXPERTS, FF, D), D ** -0.5, 0.09375, ((1, 32), (2, 32)))
    up_weight = centred(arg_keys[6], (EXPERTS, FF, D), D ** -0.5, 0.09375, ((1, 32), (2, 32)))
    down_weight = centred(arg_keys[7], (EXPERTS, FF, D), FF ** -0.5, 0.15625, ((1, 32), (2, 32)))
    return dict(rows_in=rows_in, out_grad=out_grad, route_weight=route_weight, live_rows=live_rows, expert_of_group=expert_of_group, gate_weight=gate_weight, up_weight=up_weight, down_weight=down_weight)


def block_sum(left_rows, right_rows):
    count = left_rows.shape[0]
    columns = right_rows.shape[0]
    width = left_rows.shape[1] // N_DP
    left_blocks = left_rows.reshape(count, N_DP, width).astype(jnp.float32)
    right_blocks = right_rows.reshape(columns, N_DP, width).astype(jnp.float32)
    partial_blocks = jnp.einsum('rkd,fkd->krf', left_blocks, right_blocks).astype(jnp.bfloat16)
    partial_blocks = lax.optimization_barrier(partial_blocks)
    return jnp.sum(partial_blocks.astype(jnp.float32), axis=0)


def reference(rows_in, out_grad, route_weight, live_rows, expert_of_group, gate_weight, up_weight, down_weight):
    def one_group(entry_pair):
        row_block, grad_block, weight_block, live_count, expert = entry_pair
        w_gate = gate_weight[expert]
        w_up = up_weight[expert]
        w_down = down_weight[expert]
        position = jnp.arange(ROWS, dtype=jnp.int32)
        live_mask = (position < live_count).astype(jnp.float32)
        scaled = (grad_block.astype(jnp.float32) * (weight_block * live_mask)[:, None]).astype(jnp.bfloat16)
        gate_sum = block_sum(row_block, w_gate)
        up_sum = block_sum(row_block, w_up)
        hidden_grad = block_sum(scaled, w_down)
        sigmoid_gate = jax.nn.sigmoid(gate_sum)
        activated = gate_sum * sigmoid_gate
        hidden_act = (activated * up_sum).astype(jnp.bfloat16)
        up_rows_grad = (hidden_grad * activated).astype(jnp.bfloat16)
        gate_rows_grad = (hidden_grad * up_sum * sigmoid_gate * (1.0 + gate_sum * (1.0 - sigmoid_gate))).astype(jnp.bfloat16)
        rows_grad = (jnp.dot(gate_rows_grad, w_gate, preferred_element_type=jnp.float32)
                     + jnp.dot(up_rows_grad, w_up, preferred_element_type=jnp.float32)).astype(jnp.bfloat16)
        term_gate = jnp.dot(gate_rows_grad.T, row_block, preferred_element_type=jnp.float32).astype(jnp.bfloat16)
        term_up = jnp.dot(up_rows_grad.T, row_block, preferred_element_type=jnp.float32).astype(jnp.bfloat16)
        term_down = jnp.dot(hidden_act.T, scaled, preferred_element_type=jnp.float32).astype(jnp.bfloat16)
        return rows_grad, term_gate, term_up, term_down

    inputs = (rows_in.reshape(GROUPS, ROWS, D), out_grad.reshape(GROUPS, ROWS, D),
              route_weight.reshape(GROUPS, ROWS), live_rows, expert_of_group)
    rows_grad, terms_gate, terms_up, terms_down = lax.map(one_group, inputs)

    def expert_totals(contribs):
        def accumulate(running, entry_pair):
            expert, contrib = entry_pair
            current = lax.dynamic_index_in_dim(running, expert, 0, keepdims=False)
            running = lax.dynamic_update_index_in_dim(running, current + contrib.astype(jnp.float32), expert, 0)
            return running, None
        running, _ = lax.scan(accumulate, jnp.zeros((EXPERTS, FF, D), jnp.float32), (expert_of_group, contribs))
        return running.astype(jnp.bfloat16)

    gate_grad = expert_totals(terms_gate)
    up_grad = expert_totals(terms_up)
    down_grad = expert_totals(terms_down)
    return rows_grad.reshape(RTOTAL, D), gate_grad, up_grad, down_grad
```

```python
import jax
import jax.numpy as jnp
from jax import lax
from jax.sharding import PartitionSpec as P


def product(left_rows, right_rows):
    return jnp.einsum("rd,fd->rf", left_rows, right_rows, preferred_element_type=jnp.float32)


def shards(
    rows_in, out_grad, route_weight, live_rows, expert_of_group, gate_weight, up_weight, down_weight
):
    groups = lax.axis_size("expert")
    n_dp = lax.axis_size("dp")
    chips = n_dp // 2
    experts_all, unit_piece, piece_width = gate_weight.shape
    units_all = unit_piece * groups
    row_count = rows_in.shape[0]
    half = row_count // 2
    share = half // chips
    core = lax.axis_index("dp") % 2
    partners = [(i, i ^ 1) for i in range(n_dp)]
    same_core = [[2 * i + c for i in range(chips)] for c in range(2)]

    outgoing = jnp.stack(
        [
            gate_weight[expert_of_group],
            up_weight[expert_of_group],
            down_weight[expert_of_group],
        ],
        axis=1,
    ).reshape(groups, 3 * unit_piece, piece_width)
    fetched = lax.all_to_all(outgoing, "expert", split_axis=0, concat_axis=0, tiled=True)
    fetched = fetched.reshape(groups, 3, unit_piece, piece_width)
    w_gate, w_up, w_down = (fetched[:, m].reshape(units_all, piece_width) for m in range(3))

    position = jnp.arange(row_count, dtype=jnp.int32)
    live_mask = (position < live_rows[0]).astype(jnp.float32)
    scaled = (out_grad.astype(jnp.float32) * (route_weight * live_mask)[:, None]).astype(
        jnp.bfloat16
    )

    def half_of(rows, which):
        return lax.dynamic_slice_in_dim(rows, which * half, half, axis=0)

    rows_mine, rows_other = half_of(rows_in, core), half_of(rows_in, 1 - core)
    scaled_mine, scaled_other = half_of(scaled, core), half_of(scaled, 1 - core)

    sent = jnp.concatenate(
        [
            product(rows_other, w_gate).astype(jnp.bfloat16),
            product(rows_other, w_up).astype(jnp.bfloat16),
            product(scaled_other, w_down).astype(jnp.bfloat16),
        ],
        axis=1,
    )
    got = lax.ppermute(sent, "dp", partners)
    got = [got[:, m * units_all : (m + 1) * units_all].astype(jnp.float32) for m in range(3)]
    paired = jnp.concatenate(
        [
            (product(rows_mine, w_gate) + got[0]).astype(jnp.bfloat16),
            (product(rows_mine, w_up) + got[1]).astype(jnp.bfloat16),
            (product(scaled_mine, w_down) + got[2]).astype(jnp.bfloat16),
        ],
        axis=1,
    ).reshape(chips, share, 3 * units_all)
    parts = lax.all_to_all(
        paired, "dp", split_axis=0, concat_axis=0, tiled=True, axis_index_groups=same_core
    )
    sums = jnp.sum(parts.astype(jnp.float32), axis=0)
    gate_sum, up_sum, hidden_grad = (
        sums[:, m * units_all : (m + 1) * units_all] for m in range(3)
    )
    sigmoid_gate = jax.nn.sigmoid(gate_sum)
    activated = gate_sum * sigmoid_gate
    hidden = jnp.concatenate(
        [
            hidden_grad * up_sum * sigmoid_gate * (1.0 + gate_sum * (1.0 - sigmoid_gate)),
            hidden_grad * activated,
            activated * up_sum,
        ],
        axis=1,
    ).astype(jnp.bfloat16)

    copies = jnp.broadcast_to(hidden[None], (chips, share, 3 * units_all))
    hidden_mine = lax.all_to_all(
        copies, "dp", split_axis=0, concat_axis=0, tiled=True, axis_index_groups=same_core
    ).reshape(half, 3 * units_all)
    hidden_other = lax.ppermute(hidden_mine, "dp", partners)

    def parts_of(hidden_half):
        return tuple(hidden_half[:, m * units_all : (m + 1) * units_all] for m in range(3))

    def term(mine, other, left, right):
        total = jnp.einsum("rf,rd->fd", mine, left, preferred_element_type=jnp.float32)
        total += jnp.einsum("rf,rd->fd", other, right, preferred_element_type=jnp.float32)
        return total.astype(jnp.bfloat16).reshape(groups, unit_piece, piece_width)

    gate_mine, up_mine, act_mine = parts_of(hidden_mine)
    gate_other, up_other, act_other = parts_of(hidden_other)
    terms = jnp.concatenate(
        [
            term(gate_mine, gate_other, rows_mine, rows_other),
            term(up_mine, up_other, rows_mine, rows_other),
            term(act_mine, act_other, scaled_mine, scaled_other),
        ],
        axis=1,
    )
    returned = lax.all_to_all(terms, "expert", split_axis=0, concat_axis=0, tiled=True)
    returned = returned.reshape(groups, 3, unit_piece, piece_width)

    def rows_grad_of(gate_half, up_half):
        return (
            jnp.dot(gate_half, w_gate, preferred_element_type=jnp.float32)
            + jnp.dot(up_half, w_up, preferred_element_type=jnp.float32)
        ).astype(jnp.bfloat16)

    grad_mine = rows_grad_of(gate_mine, up_mine)
    grad_other = rows_grad_of(gate_other, up_other)
    first = jnp.where(core == 0, grad_mine, grad_other)
    second = jnp.where(core == 0, grad_other, grad_mine)
    rows_grad = jnp.concatenate([first, second], axis=0)

    owner_table = (
        expert_of_group[:, None] == jnp.arange(experts_all, dtype=jnp.int32)[None, :]
    ).astype(jnp.bfloat16)
    gate_grad, up_grad, down_grad = (
        jnp.einsum(
            "ge,gfd->efd", owner_table, returned[:, m], preferred_element_type=jnp.float32
        ).astype(jnp.bfloat16)
        for m in range(3)
    )
    return (rows_grad, gate_grad, up_grad, down_grad)


def solution(mesh):
    return jax.shard_map(
        shards,
        mesh=mesh,
        in_specs=(
            P("expert", "dp"),
            P("expert", "dp"),
            P("expert"),
            P("expert"),
            P(),
            P(None, "expert", "dp"),
            P(None, "expert", "dp"),
            P(None, "expert", "dp"),
        ),
        out_specs=(
            P("expert", "dp"),
            P(None, "expert", "dp"),
            P(None, "expert", "dp"),
            P(None, "expert", "dp"),
        ),
        check_vma=False,
    )
```

```python
import functools

import jax
import jax.numpy as jnp
from jax import lax
from jax.experimental import pallas as pl
from jax.experimental.pallas import tpu as pltpu
from jax.sharding import PartitionSpec as P

LANES = 128
VMEM_LIMIT = 48 * 1024 * 1024


def product(left_rows, right_rows):
    return jnp.einsum("rd,fd->rf", left_rows, right_rows, preferred_element_type=jnp.float32)


def over_first(left, right):
    return lax.dot_general(
        left, right, (((0,), (0,)), ((), ())), preferred_element_type=jnp.float32
    )


def hidden_kernel(groups, piece, parts_ref, pieces_ref, grads_ref):
    units = groups * piece
    sums = parts_ref[0].astype(jnp.float32)
    for chip in range(1, parts_ref.shape[0]):
        sums += parts_ref[chip].astype(jnp.float32)
    gate_sum, up_sum, hidden_grad = (sums[:, m * units : (m + 1) * units] for m in range(3))
    sigmoid_gate = 1.0 / (1.0 + jnp.exp(-gate_sum))
    activated = gate_sum * sigmoid_gate
    hidden_act = activated * up_sum
    up_rows_grad = hidden_grad * activated
    gate_rows_grad = hidden_grad * up_sum * sigmoid_gate * (1.0 + gate_sum * (1.0 - sigmoid_gate))
    grads_ref[:, :units] = gate_rows_grad.astype(grads_ref.dtype)
    grads_ref[:, units:] = up_rows_grad.astype(grads_ref.dtype)
    spare = jnp.zeros((gate_sum.shape[0], 2 * LANES - 3 * piece), jnp.float32)
    for holder in range(groups):
        cut = slice(holder * piece, (holder + 1) * piece)
        pieces_ref[holder] = jnp.concatenate(
            [gate_rows_grad[:, cut], up_rows_grad[:, cut], hidden_act[:, cut], spare], axis=1
        ).astype(pieces_ref.dtype)


def pack_kernel(groups, tail, pieces_ref, packed_ref):
    per = LANES // tail
    packed_ref[:groups] = pieces_ref[:, :, :LANES]
    for block in range(groups // per):
        packed_ref[groups + block] = jnp.concatenate(
            [
                pieces_ref[block * per + k, :, LANES : LANES + tail].astype(jnp.float32)
                for k in range(per)
            ],
            axis=1,
        ).astype(packed_ref.dtype)


def weight_kernel(
    piece,
    tail,
    expert_ref,
    core_ref,
    rows_mine_ref,
    rows_other_ref,
    main_mine_ref,
    main_other_ref,
    rest_mine_ref,
    rest_other_ref,
    gate_ref,
    up_ref,
    down_ref,
    total_ref,
):
    step = pl.program_id(0)
    per = main_mine_ref.shape[1]
    half = rows_mine_ref.shape[2]

    @pl.when(step == 0)
    def _():
        total_ref[...] = jnp.zeros_like(total_ref)

    rest_mine = rest_mine_ref[:, 0].reshape(half, LANES)
    rest_other = rest_other_ref[:, 0].reshape(half, LANES)
    for k in range(per):
        expert = expert_ref[step * per + k]
        rows_mine, rows_other = rows_mine_ref[k, 0], rows_other_ref[k, 0]
        main = over_first(main_mine_ref[:, k].reshape(half, LANES), rows_mine)
        main += over_first(main_other_ref[:, k].reshape(half, LANES), rows_other)
        rest = over_first(rest_mine, rows_mine[:, LANES:])
        rest += over_first(rest_other, rows_other[:, LANES:])
        total_ref[expert, : 2 * piece] += main[: 2 * piece, :LANES]
        total_ref[expert, 2 * piece : LANES] += main[2 * piece :, LANES:]
        total_ref[expert, LANES:] += rest[k * tail : (k + 1) * tail]

    @pl.when(step == pl.num_programs(0) - 1)
    def _():
        gate_ref[...] = total_ref[:, :piece].astype(gate_ref.dtype)
        up_ref[...] = total_ref[:, piece : 2 * piece].astype(up_ref.dtype)
        down_ref[...] = total_ref[:, 2 * piece :].astype(down_ref.dtype)


def shards(
    rows_in, out_grad, route_weight, live_rows, expert_of_group, gate_weight, up_weight, down_weight
):
    groups = lax.axis_size("expert")
    n_dp = lax.axis_size("dp")
    chips = n_dp // 2
    experts_all, unit_piece, piece_width = gate_weight.shape
    units_all = unit_piece * groups
    row_count = rows_in.shape[0]
    half = row_count // 2
    share = half // chips
    tail = 3 * unit_piece - LANES
    per = LANES // tail
    core = lax.axis_index("dp") % 2
    partners = [(i, i ^ 1) for i in range(n_dp)]
    same_core = [[2 * i + c for i in range(chips)] for c in range(2)]

    def among_chips(blocks):
        return lax.all_to_all(
            blocks, "dp", split_axis=0, concat_axis=0, tiled=True, axis_index_groups=same_core
        )

    outgoing = jnp.stack(
        [
            gate_weight[expert_of_group],
            up_weight[expert_of_group],
            down_weight[expert_of_group],
        ],
        axis=1,
    ).reshape(groups, 3 * unit_piece, piece_width)
    fetched = lax.all_to_all(outgoing, "expert", split_axis=0, concat_axis=0, tiled=True)

    position = jnp.arange(row_count, dtype=jnp.int32)
    live_mask = (position < live_rows[0]).astype(jnp.float32)
    scaled = (out_grad.astype(jnp.float32) * (route_weight * live_mask)[:, None]).astype(
        jnp.bfloat16
    )
    both = jnp.concatenate([rows_in, scaled], axis=1)
    both, fetched = lax.optimization_barrier((both, fetched))
    rows_all = lax.all_gather(both, "expert", axis=0, tiled=True)
    fetched = fetched.reshape(groups, 3, unit_piece, piece_width)
    w_gate, w_up, w_down = (fetched[:, m].reshape(units_all, piece_width) for m in range(3))

    def half_of(rows, which):
        return lax.dynamic_slice_in_dim(rows, which * half, half, axis=0)

    rows_mine, rows_other = half_of(rows_in, core), half_of(rows_in, 1 - core)
    scaled_mine, scaled_other = half_of(scaled, core), half_of(scaled, 1 - core)

    sent = jnp.concatenate(
        [
            product(rows_other, w_gate).astype(jnp.bfloat16),
            product(rows_other, w_up).astype(jnp.bfloat16),
            product(scaled_other, w_down).astype(jnp.bfloat16),
        ],
        axis=1,
    )
    got = lax.ppermute(sent, "dp", partners)
    got = [got[:, m * units_all : (m + 1) * units_all].astype(jnp.float32) for m in range(3)]
    paired = jnp.concatenate(
        [
            (product(rows_mine, w_gate) + got[0]).astype(jnp.bfloat16),
            (product(rows_mine, w_up) + got[1]).astype(jnp.bfloat16),
            (product(scaled_mine, w_down) + got[2]).astype(jnp.bfloat16),
        ],
        axis=1,
    ).reshape(chips, share, 3 * units_all)
    parts = among_chips(paired)
    pieces, grads = pl.pallas_call(
        functools.partial(hidden_kernel, groups, unit_piece),
        out_shape=(
            jax.ShapeDtypeStruct((groups, share, 2 * LANES), jnp.bfloat16),
            jax.ShapeDtypeStruct((share, 2 * units_all), jnp.bfloat16),
        ),
        compiler_params=pltpu.CompilerParams(vmem_limit_bytes=VMEM_LIMIT),
    )(parts)

    pieces = lax.all_to_all(pieces, "expert", split_axis=0, concat_axis=0, tiled=True)
    packed_count = groups + groups // per
    packed = pl.pallas_call(
        functools.partial(pack_kernel, groups, tail),
        out_shape=jax.ShapeDtypeStruct((packed_count, share, LANES), jnp.bfloat16),
        compiler_params=pltpu.CompilerParams(vmem_limit_bytes=VMEM_LIMIT),
    )(pieces)
    packed_mine = among_chips(
        jnp.broadcast_to(packed[None], (chips, packed_count, share, LANES))
    )
    packed_other = lax.ppermute(packed_mine, "dp", partners)

    rows_by_half = rows_all.reshape(groups, 2, half, 2 * piece_width)
    main_spec = pl.BlockSpec((chips, per, share, LANES), lambda i, e, c: (0, i, 0, 0))
    rest_spec = pl.BlockSpec((chips, 1, share, LANES), lambda i, e, c: (0, groups + i, 0, 0))
    grad_shape = (experts_all, unit_piece, piece_width)
    grad_spec = pl.BlockSpec(grad_shape, lambda i, e, c: (0, 0, 0))
    gate_grad, up_grad, down_grad = pl.pallas_call(
        functools.partial(weight_kernel, unit_piece, tail),
        grid_spec=pltpu.PrefetchScalarGridSpec(
            num_scalar_prefetch=2,
            grid=(groups // per,),
            in_specs=[
                pl.BlockSpec((per, 1, half, 2 * piece_width), lambda i, e, c: (i, c[0], 0, 0)),
                pl.BlockSpec((per, 1, half, 2 * piece_width), lambda i, e, c: (i, 1 - c[0], 0, 0)),
                main_spec,
                main_spec,
                rest_spec,
                rest_spec,
            ],
            out_specs=(grad_spec, grad_spec, grad_spec),
            scratch_shapes=[
                pltpu.VMEM((experts_all, 3 * unit_piece, piece_width), jnp.float32)
            ],
        ),
        out_shape=tuple(jax.ShapeDtypeStruct(grad_shape, jnp.bfloat16) for _ in range(3)),
        compiler_params=pltpu.CompilerParams(vmem_limit_bytes=VMEM_LIMIT),
        cost_estimate=pl.CostEstimate(
            flops=4 * groups * row_count * LANES * 3 * LANES,
            bytes_accessed=16 * 1024 * 1024,
            transcendentals=0,
        ),
    )(
        expert_of_group,
        core.reshape(1).astype(jnp.int32),
        rows_by_half,
        rows_by_half,
        packed_mine,
        packed_other,
        packed_mine,
        packed_other,
    )

    grads_mine = among_chips(
        jnp.broadcast_to(grads[None], (chips, share, 2 * units_all))
    ).reshape(half, 2 * units_all)
    grads_other = lax.ppermute(grads_mine, "dp", partners)

    def rows_grad_of(grads_half):
        return (
            jnp.dot(grads_half[:, :units_all], w_gate, preferred_element_type=jnp.float32)
            + jnp.dot(grads_half[:, units_all:], w_up, preferred_element_type=jnp.float32)
        ).astype(jnp.bfloat16)

    grad_mine, grad_other = rows_grad_of(grads_mine), rows_grad_of(grads_other)
    first = jnp.where(core == 0, grad_mine, grad_other)
    second = jnp.where(core == 0, grad_other, grad_mine)
    rows_grad = jnp.concatenate([first, second], axis=0)
    return (rows_grad, gate_grad, up_grad, down_grad)


def solution(mesh):
    return jax.shard_map(
        shards,
        mesh=mesh,
        in_specs=(
            P("expert", "dp"),
            P("expert", "dp"),
            P("expert"),
            P("expert"),
            P(),
            P(None, "expert", "dp"),
            P(None, "expert", "dp"),
            P(None, "expert", "dp"),
        ),
        out_specs=(
            P("expert", "dp"),
            P(None, "expert", "dp"),
            P(None, "expert", "dp"),
            P(None, "expert", "dp"),
        ),
        check_vma=False,
    )
```

```python
import functools

import jax
import jax.numpy as jnp
from jax import lax
from jax.experimental import pallas as pl
from jax.experimental.pallas import tpu as pltpu
from jax.sharding import PartitionSpec as P

LANES = 128
VMEM_LIMIT = 20 * 1024 * 1024
LARGE_VMEM_LIMIT = 60 * 1024 * 1024


def over_first(left, right):
    return lax.dot_general(
        left, right, (((0,), (0,)), ((), ())), preferred_element_type=jnp.float32
    )


def gather_kernel(piece, expert_ref, gate_ref, up_ref, down_ref, out_ref, sems):
    copies = []
    for group in range(out_ref.shape[0]):
        for m, weight_ref in enumerate((gate_ref, up_ref, down_ref)):
            copy = pltpu.make_async_copy(
                weight_ref.at[expert_ref[group]],
                out_ref.at[group, pl.ds(m * piece, piece)],
                sems.at[group * 3 + m],
            )
            copy.start()
            copies.append(copy)
    for copy in copies:
        copy.wait()


def flat(weights_ref, m, piece):
    groups, _, width = weights_ref.shape
    return weights_ref[:, m * piece : (m + 1) * piece, :].reshape(groups * piece, width)


def products(piece, which, rows_ref, scaled_ref, weights_ref):
    half = rows_ref.shape[0] // 2
    start = pl.multiple_of(which * half, half)
    rows, scaled = rows_ref[pl.ds(start, half)], scaled_ref[pl.ds(start, half)]
    for m, left in enumerate((rows, rows, scaled)):
        yield m, lax.dot_general(
            left,
            flat(weights_ref, m, piece),
            (((1,), (1,)), ((), ())),
            preferred_element_type=jnp.float32,
        )


def sent_kernel(piece, core_ref, rows_ref, scaled_ref, weights_ref, out_ref):
    units = out_ref.shape[1] // 3
    for m, summed in products(piece, 1 - core_ref[0], rows_ref, scaled_ref, weights_ref):
        out_ref[:, m * units : (m + 1) * units] = summed.astype(out_ref.dtype)


def paired_kernel(piece, core_ref, rows_ref, scaled_ref, weights_ref, got_ref, out_ref):
    units = out_ref.shape[1] // 3
    for m, summed in products(piece, core_ref[0], rows_ref, scaled_ref, weights_ref):
        cut = slice(m * units, (m + 1) * units)
        out_ref[:, cut] = (summed + got_ref[:, cut].astype(jnp.float32)).astype(out_ref.dtype)


def hidden_kernel(groups, piece, parts_ref, pieces_ref, grads_ref):
    units = groups * piece
    sums = parts_ref[0].astype(jnp.float32)
    for chip in range(1, parts_ref.shape[0]):
        sums += parts_ref[chip].astype(jnp.float32)
    gate_sum, up_sum, hidden_grad = (sums[:, m * units : (m + 1) * units] for m in range(3))
    sigmoid_gate = 1.0 / (1.0 + jnp.exp(-gate_sum))
    activated = gate_sum * sigmoid_gate
    hidden_act = activated * up_sum
    up_rows_grad = hidden_grad * activated
    gate_rows_grad = hidden_grad * up_sum * sigmoid_gate * (1.0 + gate_sum * (1.0 - sigmoid_gate))
    blocks = units // LANES
    for k in range(blocks):
        cut = slice(k * LANES, (k + 1) * LANES)
        grads_ref[k] = gate_rows_grad[:, cut].astype(grads_ref.dtype)
        grads_ref[blocks + k] = up_rows_grad[:, cut].astype(grads_ref.dtype)
    _, fold, width = pieces_ref.shape
    spare = jnp.zeros((fold, width - 6 * piece), jnp.float32)
    for holder in range(groups):
        cut = slice(holder * piece, (holder + 1) * piece)
        pieces_ref[holder] = jnp.concatenate(
            [
                array[rows, cut]
                for rows in (slice(0, fold), slice(fold, 2 * fold))
                for array in (gate_rows_grad, up_rows_grad, hidden_act)
            ]
            + [spare],
            axis=1,
        ).astype(pieces_ref.dtype)


def pack_kernel(groups, tail, pieces_ref, grads_ref, copies_ref):
    per = LANES // tail
    width = LANES + tail
    rows = []
    for group in range(groups):
        folded = pieces_ref[group].astype(jnp.float32)
        rows.append(jnp.concatenate([folded[:, :width], folded[:, width : 2 * width]], axis=0))
    for group in range(groups):
        copies_ref[0, group] = rows[group][:, :LANES].astype(copies_ref.dtype)
    for block in range(groups // per):
        copies_ref[0, groups + block] = jnp.concatenate(
            [rows[block * per + k][:, LANES:] for k in range(per)], axis=1
        ).astype(copies_ref.dtype)
    copies_ref[0, groups + groups // per :] = grads_ref[...]
    for chip in range(1, copies_ref.shape[0]):
        copies_ref[chip] = copies_ref[0]


def rows_kernel(piece, core_ref, mine_ref, other_ref, weights_ref, out_ref, total_ref):
    m = pl.program_id(0)
    half = out_ref.shape[0] // 2
    blocks = mine_ref.shape[1]
    groups, width = weights_ref.shape[0], weights_ref.shape[2]
    start = pl.multiple_of(m * piece, piece)
    weights = weights_ref[:, pl.ds(start, piece), :].reshape(groups * piece, width)
    for ref, which in ((mine_ref, core_ref[0]), (other_ref, 1 - core_ref[0])):
        total = jnp.zeros((half, width), jnp.float32)
        for k in range(blocks):
            total += jnp.dot(
                ref[:, k].reshape(half, LANES),
                weights[k * LANES : (k + 1) * LANES],
                preferred_element_type=jnp.float32,
            )
        rows = pl.ds(pl.multiple_of(which * half, half), half)

        @pl.when(m == 0)
        def _():
            total_ref[rows] = total

        @pl.when(m == 1)
        def _():
            out_ref[rows] = (total_ref[rows] + total).astype(out_ref.dtype)


def weight_kernel(
    piece,
    tail,
    expert_ref,
    core_ref,
    rows_mine_ref,
    rows_other_ref,
    main_mine_ref,
    main_other_ref,
    rest_mine_ref,
    rest_other_ref,
    gate_ref,
    up_ref,
    down_ref,
    total_ref,
):
    step = pl.program_id(0)
    per = main_mine_ref.shape[1]
    half = rows_mine_ref.shape[2]

    @pl.when(step == 0)
    def _():
        total_ref[...] = jnp.zeros_like(total_ref)

    rest_mine = rest_mine_ref[:, 0].reshape(half, LANES)
    rest_other = rest_other_ref[:, 0].reshape(half, LANES)
    for k in range(per):
        expert = expert_ref[step * per + k]
        rows_mine, rows_other = rows_mine_ref[k, 0], rows_other_ref[k, 0]
        main = over_first(main_mine_ref[:, k].reshape(half, LANES), rows_mine)
        main += over_first(main_other_ref[:, k].reshape(half, LANES), rows_other)
        rest = over_first(rest_mine, rows_mine[:, LANES:])
        rest += over_first(rest_other, rows_other[:, LANES:])
        total_ref[expert, : 2 * piece] += main[: 2 * piece, :LANES]
        total_ref[expert, 2 * piece : LANES] += main[2 * piece :, LANES:]
        total_ref[expert, LANES:] += rest[k * tail : (k + 1) * tail]

    @pl.when(step == pl.num_programs(0) - 1)
    def _():
        gate_ref[...] = total_ref[:, :piece].astype(gate_ref.dtype)
        up_ref[...] = total_ref[:, piece : 2 * piece].astype(up_ref.dtype)
        down_ref[...] = total_ref[:, 2 * piece :].astype(down_ref.dtype)


def shards(
    rows_in, out_grad, route_weight, live_rows, expert_of_group, gate_weight, up_weight, down_weight
):
    groups = lax.axis_size("expert")
    n_dp = lax.axis_size("dp")
    chips = n_dp // 2
    experts_all, unit_piece, piece_width = gate_weight.shape
    units_all = unit_piece * groups
    row_count = rows_in.shape[0]
    half = row_count // 2
    share = half // chips
    tail = 3 * unit_piece - LANES
    per = LANES // tail
    core = lax.axis_index("dp") % 2
    partners = [(i, i ^ 1) for i in range(n_dp)]
    same_core = [[2 * i + c for i in range(chips)] for c in range(2)]

    def among_chips(blocks):
        return lax.all_to_all(
            blocks, "dp", split_axis=0, concat_axis=0, tiled=True, axis_index_groups=same_core
        )

    in_vmem = pl.BlockSpec(memory_space=pltpu.VMEM)
    in_smem = pl.BlockSpec(memory_space=pltpu.SMEM)
    in_place = pl.BlockSpec(memory_space=pl.ANY)
    roomy = pltpu.CompilerParams(vmem_limit_bytes=VMEM_LIMIT)
    core_index = core.reshape(1).astype(jnp.int32)

    outgoing = pl.pallas_call(
        functools.partial(gather_kernel, unit_piece),
        in_specs=[in_smem, in_place, in_place, in_place],
        out_specs=in_vmem,
        out_shape=jax.ShapeDtypeStruct((groups, 3 * unit_piece, piece_width), jnp.bfloat16),
        scratch_shapes=[pltpu.SemaphoreType.DMA((3 * groups,))],
    )(expert_of_group, gate_weight, up_weight, down_weight)
    fetched = lax.all_to_all(outgoing, "expert", split_axis=0, concat_axis=0, tiled=True)

    position = jnp.arange(row_count, dtype=jnp.int32)
    live_mask = (position < live_rows[0]).astype(jnp.float32)
    scaled = (out_grad.astype(jnp.float32) * (route_weight * live_mask)[:, None]).astype(
        jnp.bfloat16
    )
    both = jnp.concatenate([rows_in, scaled], axis=1)
    both, fetched = lax.optimization_barrier((both, fetched))
    rows_all = lax.all_gather(both, "expert", axis=0, tiled=True)

    product_flops = 2 * half * 3 * units_all * piece_width
    product_bytes = 2 * (half + groups * piece_width) * 3 * unit_piece * 16
    sent = pl.pallas_call(
        functools.partial(sent_kernel, unit_piece),
        in_specs=[in_smem, in_vmem, in_vmem, in_vmem],
        out_specs=in_vmem,
        out_shape=jax.ShapeDtypeStruct((half, 3 * units_all), jnp.bfloat16),
        compiler_params=roomy,
        cost_estimate=pl.CostEstimate(
            flops=product_flops, bytes_accessed=product_bytes, transcendentals=0
        ),
    )(core_index, rows_in, scaled, fetched)
    got = lax.ppermute(sent, "dp", partners)
    paired = pl.pallas_call(
        functools.partial(paired_kernel, unit_piece),
        in_specs=[in_smem, in_vmem, in_vmem, in_vmem, in_vmem],
        out_specs=in_vmem,
        out_shape=jax.ShapeDtypeStruct((half, 3 * units_all), jnp.bfloat16),
        compiler_params=roomy,
        cost_estimate=pl.CostEstimate(
            flops=product_flops, bytes_accessed=product_bytes, transcendentals=0
        ),
    )(core_index, rows_in, scaled, fetched, got).reshape(chips, share, 3 * units_all)
    parts = among_chips(paired)
    grad_blocks = 2 * units_all // LANES
    pieces, grads = pl.pallas_call(
        functools.partial(hidden_kernel, groups, unit_piece),
        out_shape=(
            jax.ShapeDtypeStruct((groups, share // 2, 3 * LANES), jnp.bfloat16),
            jax.ShapeDtypeStruct((grad_blocks, share, LANES), jnp.bfloat16),
        ),
        compiler_params=roomy,
    )(parts)

    pieces = lax.all_to_all(pieces, "expert", split_axis=0, concat_axis=0, tiled=True)
    packed_count = groups + groups // per
    copies = pl.pallas_call(
        functools.partial(pack_kernel, groups, tail),
        out_shape=jax.ShapeDtypeStruct(
            (chips, packed_count + grad_blocks, share, LANES), jnp.bfloat16
        ),
        compiler_params=roomy,
    )(pieces, grads)
    hidden_mine = among_chips(copies)
    hidden_other = lax.ppermute(hidden_mine, "dp", partners)

    gate_blocks = grad_blocks // 2
    first = packed_count // gate_blocks
    grads_spec = pl.BlockSpec(
        (chips, gate_blocks, share, LANES), lambda m, c: (0, first + m, 0, 0)
    )
    rows_grad = pl.pallas_call(
        functools.partial(rows_kernel, unit_piece),
        grid_spec=pltpu.PrefetchScalarGridSpec(
            num_scalar_prefetch=1,
            grid=(2,),
            in_specs=[
                grads_spec,
                grads_spec,
                pl.BlockSpec(fetched.shape, lambda m, c: (0, 0, 0)),
            ],
            out_specs=pl.BlockSpec((row_count, piece_width), lambda m, c: (0, 0)),
            scratch_shapes=[pltpu.VMEM((row_count, piece_width), jnp.float32)],
        ),
        out_shape=jax.ShapeDtypeStruct((row_count, piece_width), jnp.bfloat16),
        compiler_params=pltpu.CompilerParams(vmem_limit_bytes=LARGE_VMEM_LIMIT),
        cost_estimate=pl.CostEstimate(
            flops=4 * row_count * units_all * piece_width,
            bytes_accessed=5 * 1024 * 1024,
            transcendentals=0,
        ),
    )(core_index, hidden_mine, hidden_other, fetched)

    rows_by_half = rows_all.reshape(groups, 2, half, 2 * piece_width)
    main_spec = pl.BlockSpec((chips, per, share, LANES), lambda i, e, c: (0, i, 0, 0))
    rest_spec = pl.BlockSpec((chips, 1, share, LANES), lambda i, e, c: (0, groups + i, 0, 0))
    grad_shape = (experts_all, unit_piece, piece_width)
    grad_spec = pl.BlockSpec(grad_shape, lambda i, e, c: (0, 0, 0))
    gate_grad, up_grad, down_grad = pl.pallas_call(
        functools.partial(weight_kernel, unit_piece, tail),
        grid_spec=pltpu.PrefetchScalarGridSpec(
            num_scalar_prefetch=2,
            grid=(groups // per,),
            in_specs=[
                pl.BlockSpec((per, 1, half, 2 * piece_width), lambda i, e, c: (i, c[0], 0, 0)),
                pl.BlockSpec((per, 1, half, 2 * piece_width), lambda i, e, c: (i, 1 - c[0], 0, 0)),
                main_spec,
                main_spec,
                rest_spec,
                rest_spec,
            ],
            out_specs=(grad_spec, grad_spec, grad_spec),
            scratch_shapes=[
                pltpu.VMEM((experts_all, 3 * unit_piece, piece_width), jnp.float32)
            ],
        ),
        out_shape=tuple(jax.ShapeDtypeStruct(grad_shape, jnp.bfloat16) for _ in range(3)),
        compiler_params=pltpu.CompilerParams(vmem_limit_bytes=LARGE_VMEM_LIMIT),
        cost_estimate=pl.CostEstimate(
            flops=4 * groups * row_count * LANES * 3 * LANES,
            bytes_accessed=16 * 1024 * 1024,
            transcendentals=0,
        ),
    )(
        expert_of_group,
        core_index,
        rows_by_half,
        rows_by_half,
        hidden_mine,
        hidden_other,
        hidden_mine,
        hidden_other,
    )

    return (rows_grad, gate_grad, up_grad, down_grad)


def solution(mesh):
    return jax.shard_map(
        shards,
        mesh=mesh,
        in_specs=(
            P("expert", "dp"),
            P("expert", "dp"),
            P("expert"),
            P("expert"),
            P(),
            P(None, "expert", "dp"),
            P(None, "expert", "dp"),
            P(None, "expert", "dp"),
        ),
        out_specs=(
            P("expert", "dp"),
            P(None, "expert", "dp"),
            P(None, "expert", "dp"),
            P(None, "expert", "dp"),
        ),
        check_vma=False,
    )
```

```python
import functools

import jax
import jax.numpy as jnp
from jax import lax
from jax.experimental import pallas as pl
from jax.experimental.pallas import tpu as pltpu
from jax.sharding import PartitionSpec as P

LANES = 128
VMEM_LIMIT = 20 * 1024 * 1024
LARGE_VMEM_LIMIT = 50 * 1024 * 1024
GATHER_VMEM_LIMIT = 60 * 1024 * 1024


def over_first(left, right):
    return lax.dot_general(
        left, right, (((0,), (0,)), ((), ())), preferred_element_type=jnp.float32
    )


def gather_kernel(piece, expert_ref, gate_ref, up_ref, down_ref, out_ref, weights_ref, sems):
    copies = [
        pltpu.make_async_copy(weight_ref, weights_ref.at[m], sems.at[m])
        for m, weight_ref in enumerate((gate_ref, up_ref, down_ref))
    ]
    for copy in copies:
        copy.start()
    for m, copy in enumerate(copies):
        copy.wait()
        for group in range(out_ref.shape[0]):
            out_ref[group, m * piece : (m + 1) * piece] = weights_ref[m, expert_ref[group]]


def flat(weights_ref, m, piece):
    groups, _, width = weights_ref.shape
    return weights_ref[:, m * piece : (m + 1) * piece, :].reshape(groups * piece, width)


def products(piece, which, rows_ref, scaled_ref, weights_ref):
    half = rows_ref.shape[0] // 2
    start = pl.multiple_of(which * half, half)
    rows, scaled = rows_ref[pl.ds(start, half)], scaled_ref[pl.ds(start, half)]
    for m, left in enumerate((rows, rows, scaled)):
        yield m, lax.dot_general(
            left,
            flat(weights_ref, m, piece),
            (((1,), (1,)), ((), ())),
            preferred_element_type=jnp.float32,
        )


def sent_kernel(piece, core_ref, rows_ref, scaled_ref, weights_ref, out_ref):
    units = out_ref.shape[1] // 3
    for m, summed in products(piece, 1 - core_ref[0], rows_ref, scaled_ref, weights_ref):
        out_ref[:, m * units : (m + 1) * units] = summed.astype(out_ref.dtype)


def paired_kernel(piece, core_ref, rows_ref, scaled_ref, weights_ref, got_ref, out_ref):
    units = out_ref.shape[1] // 3
    for m, summed in products(piece, core_ref[0], rows_ref, scaled_ref, weights_ref):
        cut = slice(m * units, (m + 1) * units)
        out_ref[:, cut] = (summed + got_ref[:, cut].astype(jnp.float32)).astype(out_ref.dtype)


def hidden_kernel(groups, piece, parts_ref, pieces_ref, grads_ref):
    units = groups * piece
    sums = parts_ref[0].astype(jnp.float32)
    for chip in range(1, parts_ref.shape[0]):
        sums += parts_ref[chip].astype(jnp.float32)
    gate_sum, up_sum, hidden_grad = (sums[:, m * units : (m + 1) * units] for m in range(3))
    sigmoid_gate = 1.0 / (1.0 + jnp.exp(-gate_sum))
    activated = gate_sum * sigmoid_gate
    hidden_act = activated * up_sum
    up_rows_grad = hidden_grad * activated
    gate_rows_grad = hidden_grad * up_sum * sigmoid_gate * (1.0 + gate_sum * (1.0 - sigmoid_gate))
    blocks = units // LANES
    for k in range(blocks):
        cut = slice(k * LANES, (k + 1) * LANES)
        grads_ref[k] = gate_rows_grad[:, cut].astype(grads_ref.dtype)
        grads_ref[blocks + k] = up_rows_grad[:, cut].astype(grads_ref.dtype)
    _, fold, width = pieces_ref.shape
    spare = jnp.zeros((fold, width - 6 * piece), jnp.float32)
    for holder in range(groups):
        cut = slice(holder * piece, (holder + 1) * piece)
        pieces_ref[holder] = jnp.concatenate(
            [
                array[rows, cut]
                for rows in (slice(0, fold), slice(fold, 2 * fold))
                for array in (gate_rows_grad, up_rows_grad, hidden_act)
            ]
            + [spare],
            axis=1,
        ).astype(pieces_ref.dtype)


def pack_kernel(groups, tail, pieces_ref, grads_ref, copies_ref):
    per = LANES // tail
    width = LANES + tail
    rows = []
    for group in range(groups):
        folded = pieces_ref[group].astype(jnp.float32)
        rows.append(jnp.concatenate([folded[:, :width], folded[:, width : 2 * width]], axis=0))
    for group in range(groups):
        copies_ref[0, group] = rows[group][:, :LANES].astype(copies_ref.dtype)
    for block in range(groups // per):
        copies_ref[0, groups + block] = jnp.concatenate(
            [rows[block * per + k][:, LANES:] for k in range(per)], axis=1
        ).astype(copies_ref.dtype)
    copies_ref[0, groups + groups // per :] = grads_ref[...]
    for chip in range(1, copies_ref.shape[0]):
        copies_ref[chip] = copies_ref[0]


def turned_kernel(tail, piece, hidden_ref, weights_ref, turned_ref, rows_ref):
    groups, _, half = turned_ref.shape
    per = LANES // tail
    for block in range(groups // per):
        rest = hidden_ref[:, groups + block].reshape(half, LANES).T
        for k in range(per):
            group = block * per + k
            turned_ref[group, :LANES] = hidden_ref[:, group].reshape(half, LANES).T
            turned_ref[group, LANES:] = rest[k * tail : (k + 1) * tail]
    first = groups + groups // per
    blocks = (hidden_ref.shape[1] - first) // 2
    total = jnp.zeros(rows_ref.shape, jnp.float32)
    for m in range(2):
        weights = flat(weights_ref, m, piece)
        for k in range(blocks):
            total += jnp.dot(
                hidden_ref[:, first + m * blocks + k].reshape(half, LANES),
                weights[k * LANES : (k + 1) * LANES],
                preferred_element_type=jnp.float32,
            )
    rows_ref[...] = total.astype(rows_ref.dtype)


def weight_kernel(
    piece,
    steps,
    expert_ref,
    core_ref,
    mine_ref,
    other_ref,
    rows_ref,
    gate_ref,
    up_ref,
    down_ref,
    turned_ref,
    held_ref,
    total_ref,
    sems,
):
    groups = rows_ref.shape[0]
    per = groups // steps
    sides = [
        pltpu.make_async_copy(ref, turned_ref.at[i], sems.at[steps + i])
        for i, ref in enumerate((mine_ref, other_ref))
    ]
    for copy in sides:
        copy.start()
    copies = []
    for step in range(steps):
        cut = pl.ds(step * per, per)
        copies.append(pltpu.make_async_copy(rows_ref.at[cut], held_ref.at[cut], sems.at[step]))
        copies[step].start()
    total_ref[...] = jnp.zeros_like(total_ref)
    core = core_ref[0]
    for copy in sides:
        copy.wait()
    for group in range(groups):
        if group % per == 0:
            copies[group // per].wait()
        expert = expert_ref[group]
        term = jnp.dot(
            turned_ref[0, group], held_ref[group, core], preferred_element_type=jnp.float32
        )
        term += jnp.dot(
            turned_ref[1, group], held_ref[group, 1 - core], preferred_element_type=jnp.float32
        )
        total_ref[expert, : 2 * piece] += term[: 2 * piece, :LANES]
        total_ref[expert, 2 * piece :] += term[2 * piece :, LANES:]
    for m, out_ref in enumerate((gate_ref, up_ref, down_ref)):
        out_ref[...] = total_ref[:, m * piece : (m + 1) * piece].astype(out_ref.dtype)


def shards(
    rows_in, out_grad, route_weight, live_rows, expert_of_group, gate_weight, up_weight, down_weight
):
    groups = lax.axis_size("expert")
    n_dp = lax.axis_size("dp")
    chips = n_dp // 2
    experts_all, unit_piece, piece_width = gate_weight.shape
    units_all = unit_piece * groups
    row_count = rows_in.shape[0]
    half = row_count // 2
    share = half // chips
    tail = 3 * unit_piece - LANES
    per = LANES // tail
    core = lax.axis_index("dp") % 2
    partners = [(i, i ^ 1) for i in range(n_dp)]
    same_core = [[2 * i + c for i in range(chips)] for c in range(2)]

    def among_chips(blocks):
        return lax.all_to_all(
            blocks, "dp", split_axis=0, concat_axis=0, tiled=True, axis_index_groups=same_core
        )

    in_vmem = pl.BlockSpec(memory_space=pltpu.VMEM)
    in_smem = pl.BlockSpec(memory_space=pltpu.SMEM)
    in_place = pl.BlockSpec(memory_space=pl.ANY)
    roomy = pltpu.CompilerParams(vmem_limit_bytes=VMEM_LIMIT)
    core_index = core.reshape(1).astype(jnp.int32)

    outgoing = pl.pallas_call(
        functools.partial(gather_kernel, unit_piece),
        in_specs=[in_smem, in_place, in_place, in_place],
        out_specs=in_vmem,
        out_shape=jax.ShapeDtypeStruct((groups, 3 * unit_piece, piece_width), jnp.bfloat16),
        scratch_shapes=[
            pltpu.VMEM((3, *gate_weight.shape), jnp.bfloat16),
            pltpu.SemaphoreType.DMA((3,)),
        ],
        compiler_params=pltpu.CompilerParams(vmem_limit_bytes=GATHER_VMEM_LIMIT),
    )(expert_of_group, gate_weight, up_weight, down_weight)
    fetched = lax.all_to_all(outgoing, "expert", split_axis=0, concat_axis=0, tiled=True)

    position = jnp.arange(row_count, dtype=jnp.int32)
    live_mask = (position < live_rows[0]).astype(jnp.float32)
    scaled = (out_grad.astype(jnp.float32) * (route_weight * live_mask)[:, None]).astype(
        jnp.bfloat16
    )
    both = jnp.concatenate([rows_in, scaled], axis=1)
    both, fetched = lax.optimization_barrier((both, fetched))
    rows_all = lax.all_gather(both, "expert", axis=0, tiled=True)

    product_flops = 2 * half * 3 * units_all * piece_width
    product_bytes = 2 * (half + groups * piece_width) * 3 * unit_piece * 16
    sent = pl.pallas_call(
        functools.partial(sent_kernel, unit_piece),
        in_specs=[in_smem, in_vmem, in_vmem, in_vmem],
        out_specs=in_vmem,
        out_shape=jax.ShapeDtypeStruct((half, 3 * units_all), jnp.bfloat16),
        compiler_params=roomy,
        cost_estimate=pl.CostEstimate(
            flops=product_flops, bytes_accessed=product_bytes, transcendentals=0
        ),
    )(core_index, rows_in, scaled, fetched)
    got = lax.ppermute(sent, "dp", partners)
    paired = pl.pallas_call(
        functools.partial(paired_kernel, unit_piece),
        in_specs=[in_smem, in_vmem, in_vmem, in_vmem, in_vmem],
        out_specs=in_vmem,
        out_shape=jax.ShapeDtypeStruct((half, 3 * units_all), jnp.bfloat16),
        compiler_params=roomy,
        cost_estimate=pl.CostEstimate(
            flops=product_flops, bytes_accessed=product_bytes, transcendentals=0
        ),
    )(core_index, rows_in, scaled, fetched, got).reshape(chips, share, 3 * units_all)
    parts = among_chips(paired)
    grad_blocks = 2 * units_all // LANES
    pieces, grads = pl.pallas_call(
        functools.partial(hidden_kernel, groups, unit_piece),
        out_shape=(
            jax.ShapeDtypeStruct((groups, share // 2, 3 * LANES), jnp.bfloat16),
            jax.ShapeDtypeStruct((grad_blocks, share, LANES), jnp.bfloat16),
        ),
        compiler_params=roomy,
    )(parts)

    pieces = lax.all_to_all(pieces, "expert", split_axis=0, concat_axis=0, tiled=True)
    packed_count = groups + groups // per
    copies = pl.pallas_call(
        functools.partial(pack_kernel, groups, tail),
        out_shape=jax.ShapeDtypeStruct(
            (chips, packed_count + grad_blocks, share, LANES), jnp.bfloat16
        ),
        compiler_params=roomy,
    )(pieces, grads)
    hidden_mine = among_chips(copies)
    hidden_other = lax.ppermute(hidden_mine, "dp", partners)

    def turned(hidden):
        return pl.pallas_call(
            functools.partial(turned_kernel, tail, unit_piece),
            out_shape=(
                jax.ShapeDtypeStruct((groups, 3 * unit_piece, half), jnp.bfloat16),
                jax.ShapeDtypeStruct((half, piece_width), jnp.bfloat16),
            ),
            compiler_params=roomy,
            cost_estimate=pl.CostEstimate(
                flops=2 * row_count * units_all * piece_width,
                bytes_accessed=7 * 1024 * 1024,
                transcendentals=0,
            ),
        )(hidden, fetched)

    turned_mine, grad_mine = turned(hidden_mine)
    turned_other, grad_other = turned(hidden_other)
    rows_grad = jnp.concatenate(
        [
            jnp.where(core == 0, grad_mine, grad_other),
            jnp.where(core == 0, grad_other, grad_mine),
        ],
        axis=0,
    )

    rows_by_half = rows_all.reshape(groups, 2, half, 2 * piece_width)
    grad_shape = (experts_all, unit_piece, piece_width)
    gate_grad, up_grad, down_grad = pl.pallas_call(
        functools.partial(weight_kernel, unit_piece, 8),
        in_specs=[in_smem, in_smem, in_place, in_place, in_place],
        out_specs=(in_vmem,) * 3,
        out_shape=tuple(jax.ShapeDtypeStruct(grad_shape, jnp.bfloat16) for _ in range(3)),
        scratch_shapes=[
            pltpu.VMEM((2, *turned_mine.shape), jnp.bfloat16),
            pltpu.VMEM(rows_by_half.shape, jnp.bfloat16),
            pltpu.VMEM((experts_all, 3 * unit_piece, piece_width), jnp.float32),
            pltpu.SemaphoreType.DMA((8 + 2,)),
        ],
        compiler_params=pltpu.CompilerParams(vmem_limit_bytes=LARGE_VMEM_LIMIT),
        cost_estimate=pl.CostEstimate(
            flops=4 * groups * row_count * LANES * 3 * LANES,
            bytes_accessed=12 * 1024 * 1024,
            transcendentals=0,
        ),
    )(expert_of_group, core_index, turned_mine, turned_other, rows_by_half)

    return (rows_grad, gate_grad, up_grad, down_grad)


def solution(mesh):
    return jax.shard_map(
        shards,
        mesh=mesh,
        in_specs=(
            P("expert", "dp"),
            P("expert", "dp"),
            P("expert"),
            P("expert"),
            P(),
            P(None, "expert", "dp"),
            P(None, "expert", "dp"),
            P(None, "expert", "dp"),
        ),
        out_specs=(
            P("expert", "dp"),
            P(None, "expert", "dp"),
            P(None, "expert", "dp"),
            P(None, "expert", "dp"),
        ),
        check_vma=False,
    )
```

```python
import functools

import jax
import jax.numpy as jnp
from jax import lax
from jax.experimental import pallas as pl
from jax.experimental.pallas import tpu as pltpu
from jax.sharding import PartitionSpec as P

LANES = 128
VMEM_LIMIT = 20 * 1024 * 1024
LARGE_VMEM_LIMIT = 50 * 1024 * 1024
TURNED_VMEM_LIMIT = 20 * 1024 * 1024
GATHER_VMEM_LIMIT = 60 * 1024 * 1024


def over_first(left, right):
    return lax.dot_general(
        left, right, (((0,), (0,)), ((), ())), preferred_element_type=jnp.float32
    )


def gather_kernel(
    piece, expert_ref, gate_ref, up_ref, down_ref, out_ref, weights_ref, chosen_ref, in_sems, out_sems
):
    arrivals = [
        pltpu.make_async_copy(weight_ref, weights_ref.at[m], in_sems.at[m])
        for m, weight_ref in enumerate((gate_ref, up_ref, down_ref))
    ]
    for copy in arrivals:
        copy.start()
    leavings = []
    for m, copy in enumerate(arrivals):
        copy.wait()
        for group in range(out_ref.shape[0]):
            chosen_ref[m, group] = weights_ref[m, expert_ref[group]]
        leavings.append(
            pltpu.make_async_copy(
                chosen_ref.at[m], out_ref.at[:, pl.ds(m * piece, piece)], out_sems.at[m]
            )
        )
        leavings[m].start()
    for copy in leavings:
        copy.wait()


def flat(weights_ref, m, piece):
    groups, _, width = weights_ref.shape
    return weights_ref[:, m * piece : (m + 1) * piece, :].reshape(groups * piece, width)


def products(piece, which, rows_ref, scaled_ref, weights_ref):
    half = rows_ref.shape[0] // 2
    start = pl.multiple_of(which * half, half)
    rows, scaled = rows_ref[pl.ds(start, half)], scaled_ref[pl.ds(start, half)]
    for m, left in enumerate((rows, rows, scaled)):
        yield m, lax.dot_general(
            left,
            flat(weights_ref, m, piece),
            (((1,), (1,)), ((), ())),
            preferred_element_type=jnp.float32,
        )


def sent_kernel(piece, core_ref, rows_ref, scaled_ref, weights_ref, out_ref):
    units = out_ref.shape[1] // 3
    for m, summed in products(piece, 1 - core_ref[0], rows_ref, scaled_ref, weights_ref):
        out_ref[:, m * units : (m + 1) * units] = summed.astype(out_ref.dtype)


def paired_kernel(piece, core_ref, rows_ref, scaled_ref, weights_ref, got_ref, out_ref):
    units = out_ref.shape[1] // 3
    for m, summed in products(piece, core_ref[0], rows_ref, scaled_ref, weights_ref):
        cut = slice(m * units, (m + 1) * units)
        out_ref[:, cut] = (summed + got_ref[:, cut].astype(jnp.float32)).astype(out_ref.dtype)


def hidden_kernel(groups, piece, parts_ref, pieces_ref, grads_ref):
    units = groups * piece
    sums = parts_ref[0].astype(jnp.float32)
    for chip in range(1, parts_ref.shape[0]):
        sums += parts_ref[chip].astype(jnp.float32)
    gate_sum, up_sum, hidden_grad = (sums[:, m * units : (m + 1) * units] for m in range(3))
    sigmoid_gate = 1.0 / (1.0 + jnp.exp(-gate_sum))
    activated = gate_sum * sigmoid_gate
    hidden_act = activated * up_sum
    up_rows_grad = hidden_grad * activated
    gate_rows_grad = hidden_grad * up_sum * sigmoid_gate * (1.0 + gate_sum * (1.0 - sigmoid_gate))
    blocks = units // LANES
    for k in range(blocks):
        cut = slice(k * LANES, (k + 1) * LANES)
        grads_ref[k] = gate_rows_grad[:, cut].astype(grads_ref.dtype)
        grads_ref[blocks + k] = up_rows_grad[:, cut].astype(grads_ref.dtype)
    _, fold, width = pieces_ref.shape
    spare = jnp.zeros((fold, width - 6 * piece), jnp.float32)
    for holder in range(groups):
        cut = slice(holder * piece, (holder + 1) * piece)
        pieces_ref[holder] = jnp.concatenate(
            [
                array[rows, cut]
                for rows in (slice(0, fold), slice(fold, 2 * fold))
                for array in (gate_rows_grad, up_rows_grad, hidden_act)
            ]
            + [spare],
            axis=1,
        ).astype(pieces_ref.dtype)


def pack_kernel(groups, tail, pieces_ref, grads_ref, copies_ref):
    per = LANES // tail
    width = LANES + tail
    rows = []
    for group in range(groups):
        folded = pieces_ref[group].astype(jnp.float32)
        rows.append(jnp.concatenate([folded[:, :width], folded[:, width : 2 * width]], axis=0))
    for group in range(groups):
        copies_ref[0, group] = rows[group][:, :LANES].astype(copies_ref.dtype)
    for block in range(groups // per):
        copies_ref[0, groups + block] = jnp.concatenate(
            [rows[block * per + k][:, LANES:] for k in range(per)], axis=1
        ).astype(copies_ref.dtype)
    copies_ref[0, groups + groups // per :] = grads_ref[...]
    for chip in range(1, copies_ref.shape[0]):
        copies_ref[chip] = copies_ref[0]


def turned_kernel(tail, piece, core_ref, hidden_ref, weights_ref, *refs):
    *first_ref, turned_ref, rows_ref = refs
    groups, _, half = turned_ref.shape
    per = LANES // tail
    for block in range(groups // per):
        rest = hidden_ref[:, groups + block].reshape(half, LANES).T
        for k in range(per):
            group = block * per + k
            turned_ref[group, :LANES] = hidden_ref[:, group].reshape(half, LANES).T
            turned_ref[group, LANES:] = rest[k * tail : (k + 1) * tail]
    first = groups + groups // per
    blocks = (hidden_ref.shape[1] - first) // 2
    total = jnp.zeros((half, rows_ref.shape[1]), jnp.float32)
    for m in range(2):
        weights = flat(weights_ref, m, piece)
        for k in range(blocks):
            total += jnp.dot(
                hidden_ref[:, first + m * blocks + k].reshape(half, LANES),
                weights[k * LANES : (k + 1) * LANES],
                preferred_element_type=jnp.float32,
            )
    total = total.astype(rows_ref.dtype)
    if first_ref:
        core = core_ref[0]
        rows_ref[pl.ds(pl.multiple_of(core * half, half), half)] = first_ref[0][...]
        rows_ref[pl.ds(pl.multiple_of((1 - core) * half, half), half)] = total
    else:
        rows_ref[...] = total


def weight_kernel(
    piece,
    steps,
    expert_ref,
    core_ref,
    mine_ref,
    other_ref,
    rows_ref,
    gate_ref,
    up_ref,
    down_ref,
    turned_ref,
    held_ref,
    total_ref,
    sems,
):
    groups = rows_ref.shape[0]
    per = groups // steps
    copies = []
    for step in range(steps):
        cut = pl.ds(step * per, per)
        pairs = (
            (mine_ref.at[cut], turned_ref.at[0, cut]),
            (other_ref.at[cut], turned_ref.at[1, cut]),
            (rows_ref.at[cut], held_ref.at[cut]),
        )
        copies.append(
            [
                pltpu.make_async_copy(source, target, sems.at[3 * step + i])
                for i, (source, target) in enumerate(pairs)
            ]
        )
        for copy in copies[step]:
            copy.start()
    total_ref[...] = jnp.zeros_like(total_ref)
    core = core_ref[0]
    for group in range(groups):
        if group % per == 0:
            for copy in copies[group // per]:
                copy.wait()
        expert = expert_ref[group]
        term = jnp.dot(
            turned_ref[0, group], held_ref[group, core], preferred_element_type=jnp.float32
        )
        term += jnp.dot(
            turned_ref[1, group], held_ref[group, 1 - core], preferred_element_type=jnp.float32
        )
        total_ref[expert, : 2 * piece] += term[: 2 * piece, :LANES]
        total_ref[expert, 2 * piece :] += term[2 * piece :, LANES:]
    for m, out_ref in enumerate((gate_ref, up_ref, down_ref)):
        out_ref[...] = total_ref[:, m * piece : (m + 1) * piece].astype(out_ref.dtype)


def shards(
    rows_in, out_grad, route_weight, live_rows, expert_of_group, gate_weight, up_weight, down_weight
):
    groups = lax.axis_size("expert")
    n_dp = lax.axis_size("dp")
    chips = n_dp // 2
    experts_all, unit_piece, piece_width = gate_weight.shape
    units_all = unit_piece * groups
    row_count = rows_in.shape[0]
    half = row_count // 2
    share = half // chips
    tail = 3 * unit_piece - LANES
    per = LANES // tail
    core = lax.axis_index("dp") % 2
    partners = [(i, i ^ 1) for i in range(n_dp)]
    same_core = [[2 * i + c for i in range(chips)] for c in range(2)]

    def among_chips(blocks):
        return lax.all_to_all(
            blocks, "dp", split_axis=0, concat_axis=0, tiled=True, axis_index_groups=same_core
        )

    in_vmem = pl.BlockSpec(memory_space=pltpu.VMEM)
    in_smem = pl.BlockSpec(memory_space=pltpu.SMEM)
    in_place = pl.BlockSpec(memory_space=pl.ANY)
    roomy = pltpu.CompilerParams(vmem_limit_bytes=VMEM_LIMIT)
    core_index = core.reshape(1).astype(jnp.int32)

    outgoing = pl.pallas_call(
        functools.partial(gather_kernel, unit_piece),
        in_specs=[in_smem, in_place, in_place, in_place],
        out_specs=in_place,
        out_shape=jax.ShapeDtypeStruct((groups, 3 * unit_piece, piece_width), jnp.bfloat16),
        scratch_shapes=[
            pltpu.VMEM((3, *gate_weight.shape), jnp.bfloat16),
            pltpu.VMEM((3, groups, unit_piece, piece_width), jnp.bfloat16),
            pltpu.SemaphoreType.DMA((3,)),
            pltpu.SemaphoreType.DMA((3,)),
        ],
        compiler_params=pltpu.CompilerParams(vmem_limit_bytes=GATHER_VMEM_LIMIT),
    )(expert_of_group, gate_weight, up_weight, down_weight)
    fetched = lax.all_to_all(outgoing, "expert", split_axis=0, concat_axis=0, tiled=True)

    position = jnp.arange(row_count, dtype=jnp.int32)
    live_mask = (position < live_rows[0]).astype(jnp.float32)
    scaled = (out_grad.astype(jnp.float32) * (route_weight * live_mask)[:, None]).astype(
        jnp.bfloat16
    )
    both = jnp.concatenate([rows_in, scaled], axis=1)
    both, fetched = lax.optimization_barrier((both, fetched))
    rows_all = lax.all_gather(both, "expert", axis=0, tiled=True)

    product_flops = 2 * half * 3 * units_all * piece_width
    product_bytes = 2 * (half + groups * piece_width) * 3 * unit_piece * 16
    sent = pl.pallas_call(
        functools.partial(sent_kernel, unit_piece),
        in_specs=[in_smem, in_vmem, in_vmem, in_vmem],
        out_specs=in_vmem,
        out_shape=jax.ShapeDtypeStruct((half, 3 * units_all), jnp.bfloat16),
        compiler_params=roomy,
        cost_estimate=pl.CostEstimate(
            flops=product_flops, bytes_accessed=product_bytes, transcendentals=0
        ),
    )(core_index, rows_in, scaled, fetched)
    got = lax.ppermute(sent, "dp", partners)
    paired = pl.pallas_call(
        functools.partial(paired_kernel, unit_piece),
        in_specs=[in_smem, in_vmem, in_vmem, in_vmem, in_vmem],
        out_specs=in_vmem,
        out_shape=jax.ShapeDtypeStruct((half, 3 * units_all), jnp.bfloat16),
        compiler_params=roomy,
        cost_estimate=pl.CostEstimate(
            flops=product_flops, bytes_accessed=product_bytes, transcendentals=0
        ),
    )(core_index, rows_in, scaled, fetched, got).reshape(chips, share, 3 * units_all)
    parts = among_chips(paired)
    grad_blocks = 2 * units_all // LANES
    pieces, grads = pl.pallas_call(
        functools.partial(hidden_kernel, groups, unit_piece),
        out_shape=(
            jax.ShapeDtypeStruct((groups, share // 2, 3 * LANES), jnp.bfloat16),
            jax.ShapeDtypeStruct((grad_blocks, share, LANES), jnp.bfloat16),
        ),
        compiler_params=roomy,
    )(parts)

    pieces = lax.all_to_all(pieces, "expert", split_axis=0, concat_axis=0, tiled=True)
    packed_count = groups + groups // per
    copies = pl.pallas_call(
        functools.partial(pack_kernel, groups, tail),
        out_shape=jax.ShapeDtypeStruct(
            (chips, packed_count + grad_blocks, share, LANES), jnp.bfloat16
        ),
        compiler_params=roomy,
    )(pieces, grads)
    hidden_mine = among_chips(copies)
    hidden_other = lax.ppermute(hidden_mine, "dp", partners)

    def turned(hidden, *first):
        return pl.pallas_call(
            functools.partial(turned_kernel, tail, unit_piece),
            in_specs=[in_smem] + [in_vmem] * (2 + len(first)),
            out_specs=(in_vmem, in_vmem),
            out_shape=(
                jax.ShapeDtypeStruct((groups, 3 * unit_piece, half), jnp.bfloat16),
                jax.ShapeDtypeStruct((half * (1 + len(first)), piece_width), jnp.bfloat16),
            ),
            compiler_params=pltpu.CompilerParams(vmem_limit_bytes=TURNED_VMEM_LIMIT),
            cost_estimate=pl.CostEstimate(
                flops=2 * row_count * units_all * piece_width,
                bytes_accessed=7 * 1024 * 1024,
                transcendentals=0,
            ),
        )(core_index, hidden, fetched, *first)

    turned_mine, grad_mine = turned(hidden_mine)
    turned_other, rows_grad = turned(hidden_other, grad_mine)

    rows_by_half = rows_all.reshape(groups, 2, half, 2 * piece_width)
    grad_shape = (experts_all, unit_piece, piece_width)
    gate_grad, up_grad, down_grad = pl.pallas_call(
        functools.partial(weight_kernel, unit_piece, 8),
        in_specs=[in_smem, in_smem, in_place, in_place, in_place],
        out_specs=(in_vmem,) * 3,
        out_shape=tuple(jax.ShapeDtypeStruct(grad_shape, jnp.bfloat16) for _ in range(3)),
        scratch_shapes=[
            pltpu.VMEM((2, *turned_mine.shape), jnp.bfloat16),
            pltpu.VMEM(rows_by_half.shape, jnp.bfloat16),
            pltpu.VMEM((experts_all, 3 * unit_piece, piece_width), jnp.float32),
            pltpu.SemaphoreType.DMA((3 * 8,)),
        ],
        compiler_params=pltpu.CompilerParams(vmem_limit_bytes=LARGE_VMEM_LIMIT),
        cost_estimate=pl.CostEstimate(
            flops=4 * groups * row_count * LANES * 3 * LANES,
            bytes_accessed=12 * 1024 * 1024,
            transcendentals=0,
        ),
    )(expert_of_group, core_index, turned_mine, turned_other, rows_by_half)

    return (rows_grad, gate_grad, up_grad, down_grad)


def solution(mesh):
    return jax.shard_map(
        shards,
        mesh=mesh,
        in_specs=(
            P("expert", "dp"),
            P("expert", "dp"),
            P("expert"),
            P("expert"),
            P(),
            P(None, "expert", "dp"),
            P(None, "expert", "dp"),
            P(None, "expert", "dp"),
        ),
        out_specs=(
            P("expert", "dp"),
            P(None, "expert", "dp"),
            P(None, "expert", "dp"),
            P(None, "expert", "dp"),
        ),
        check_vma=False,
    )
```

```python
import functools

import jax
import jax.numpy as jnp
from jax import lax
from jax.experimental import pallas as pl
from jax.experimental.pallas import tpu as pltpu
from jax.sharding import PartitionSpec as P

LANES = 128
VMEM_LIMIT = 20 * 1024 * 1024
LARGE_VMEM_LIMIT = 50 * 1024 * 1024
TURNED_VMEM_LIMIT = 20 * 1024 * 1024
GATHER_VMEM_LIMIT = 60 * 1024 * 1024


def over_first(left, right):
    return lax.dot_general(
        left, right, (((0,), (0,)), ((), ())), preferred_element_type=jnp.float32
    )


def gather_kernel(
    piece, expert_ref, gate_ref, up_ref, down_ref, out_ref, weights_ref, chosen_ref, in_sems, out_sems
):
    arrivals = [
        pltpu.make_async_copy(weight_ref, weights_ref.at[m], in_sems.at[m])
        for m, weight_ref in enumerate((gate_ref, up_ref, down_ref))
    ]
    for copy in arrivals:
        copy.start()
    leavings = []
    for m, copy in enumerate(arrivals):
        copy.wait()
        for group in range(out_ref.shape[0]):
            chosen_ref[m, group] = weights_ref[m, expert_ref[group]]
        leavings.append(
            pltpu.make_async_copy(
                chosen_ref.at[m], out_ref.at[:, pl.ds(m * piece, piece)], out_sems.at[m]
            )
        )
        leavings[m].start()
    for copy in leavings:
        copy.wait()


def flat(weights_ref, m, piece):
    groups, _, width = weights_ref.shape
    return weights_ref[:, m * piece : (m + 1) * piece, :].reshape(groups * piece, width)


def products(piece, which, rows_ref, scaled_ref, weights_ref):
    half = rows_ref.shape[0] // 2
    start = pl.multiple_of(which * half, half)
    rows, scaled = rows_ref[pl.ds(start, half)], scaled_ref[pl.ds(start, half)]
    for m, left in enumerate((rows, rows, scaled)):
        yield m, lax.dot_general(
            left,
            flat(weights_ref, m, piece),
            (((1,), (1,)), ((), ())),
            preferred_element_type=jnp.float32,
        )


def sent_kernel(piece, core_ref, rows_ref, scaled_ref, weights_ref, out_ref):
    units = out_ref.shape[1] // 3
    for m, summed in products(piece, 1 - core_ref[0], rows_ref, scaled_ref, weights_ref):
        out_ref[:, m * units : (m + 1) * units] = summed.astype(out_ref.dtype)


def paired_kernel(piece, core_ref, rows_ref, scaled_ref, weights_ref, got_ref, out_ref):
    units = out_ref.shape[1] // 3
    for m, summed in products(piece, core_ref[0], rows_ref, scaled_ref, weights_ref):
        cut = slice(m * units, (m + 1) * units)
        out_ref[:, cut] = (summed + got_ref[:, cut].astype(jnp.float32)).astype(out_ref.dtype)


def hidden_kernel(groups, piece, parts_ref, pieces_ref, grads_ref):
    units = groups * piece
    sums = parts_ref[0].astype(jnp.float32)
    for chip in range(1, parts_ref.shape[0]):
        sums += parts_ref[chip].astype(jnp.float32)
    gate_sum, up_sum, hidden_grad = (sums[:, m * units : (m + 1) * units] for m in range(3))
    sigmoid_gate = 1.0 / (1.0 + jnp.exp(-gate_sum))
    activated = gate_sum * sigmoid_gate
    hidden_act = activated * up_sum
    up_rows_grad = hidden_grad * activated
    gate_rows_grad = hidden_grad * up_sum * sigmoid_gate * (1.0 + gate_sum * (1.0 - sigmoid_gate))
    blocks = units // LANES
    for k in range(blocks):
        cut = slice(k * LANES, (k + 1) * LANES)
        grads_ref[k] = gate_rows_grad[:, cut].astype(grads_ref.dtype)
        grads_ref[blocks + k] = up_rows_grad[:, cut].astype(grads_ref.dtype)
    _, fold, width = pieces_ref.shape
    spare = jnp.zeros((fold, width - 6 * piece), jnp.float32)
    for holder in range(groups):
        cut = slice(holder * piece, (holder + 1) * piece)
        pieces_ref[holder] = jnp.concatenate(
            [
                array[rows, cut]
                for rows in (slice(0, fold), slice(fold, 2 * fold))
                for array in (gate_rows_grad, up_rows_grad, hidden_act)
            ]
            + [spare],
            axis=1,
        ).astype(pieces_ref.dtype)


def pack_kernel(groups, tail, pieces_ref, grads_ref, copies_ref):
    per = LANES // tail
    width = LANES + tail
    rows = []
    for group in range(groups):
        folded = pieces_ref[group].astype(jnp.float32)
        rows.append(jnp.concatenate([folded[:, :width], folded[:, width : 2 * width]], axis=0))
    for group in range(groups):
        copies_ref[0, group] = rows[group][:, :LANES].astype(copies_ref.dtype)
    for block in range(groups // per):
        copies_ref[0, groups + block] = jnp.concatenate(
            [rows[block * per + k][:, LANES:] for k in range(per)], axis=1
        ).astype(copies_ref.dtype)
    copies_ref[0, groups + groups // per :] = grads_ref[...]
    for chip in range(1, copies_ref.shape[0]):
        copies_ref[chip] = copies_ref[0]


def turned_kernel(tail, piece, core_ref, hidden_ref, weights_ref, *refs):
    *first_ref, turned_ref, rows_ref = refs
    groups, _, half = turned_ref.shape
    per = LANES // tail
    for block in range(groups // per):
        rest = hidden_ref[:, groups + block].reshape(half, LANES).T
        for k in range(per):
            group = block * per + k
            turned_ref[group, :LANES] = hidden_ref[:, group].reshape(half, LANES).T
            turned_ref[group, LANES:] = rest[k * tail : (k + 1) * tail]
    first = groups + groups // per
    blocks = (hidden_ref.shape[1] - first) // 2
    total = jnp.zeros((half, rows_ref.shape[1]), jnp.float32)
    for m in range(2):
        weights = flat(weights_ref, m, piece)
        for k in range(blocks):
            total += jnp.dot(
                hidden_ref[:, first + m * blocks + k].reshape(half, LANES),
                weights[k * LANES : (k + 1) * LANES],
                preferred_element_type=jnp.float32,
            )
    total = total.astype(rows_ref.dtype)
    if first_ref:
        core = core_ref[0]
        rows_ref[pl.ds(pl.multiple_of(core * half, half), half)] = first_ref[0][...]
        rows_ref[pl.ds(pl.multiple_of((1 - core) * half, half), half)] = total
    else:
        rows_ref[...] = total


def weight_kernel(
    piece,
    steps,
    expert_ref,
    core_ref,
    mine_ref,
    other_ref,
    rows_ref,
    gate_ref,
    up_ref,
    down_ref,
    turned_ref,
    held_ref,
    total_ref,
    sems,
):
    groups, _, half, _ = rows_ref.shape
    per = groups // steps
    core = core_ref[0]
    copies = []
    for step in range(steps):
        cut = pl.ds(step * per, per)
        pairs = (
            (mine_ref.at[cut], turned_ref.at[cut, :, pl.ds(0, half)]),
            (other_ref.at[cut], turned_ref.at[cut, :, pl.ds(half, half)]),
            (rows_ref.at[cut, core], held_ref.at[cut, pl.ds(0, half)]),
            (rows_ref.at[cut, 1 - core], held_ref.at[cut, pl.ds(half, half)]),
        )
        copies.append(
            [
                pltpu.make_async_copy(source, target, sems.at[4 * step + i])
                for i, (source, target) in enumerate(pairs)
            ]
        )
        for copy in copies[step]:
            copy.start()
    total_ref[...] = jnp.zeros_like(total_ref)
    for group in range(groups):
        if group % per == 0:
            for copy in copies[group // per]:
                copy.wait()
        expert = expert_ref[group]
        term = jnp.dot(turned_ref[group], held_ref[group], preferred_element_type=jnp.float32)
        total_ref[expert, : 2 * piece] += term[: 2 * piece, :LANES]
        total_ref[expert, 2 * piece :] += term[2 * piece :, LANES:]
    for m, out_ref in enumerate((gate_ref, up_ref, down_ref)):
        out_ref[...] = total_ref[:, m * piece : (m + 1) * piece].astype(out_ref.dtype)


def shards(
    rows_in, out_grad, route_weight, live_rows, expert_of_group, gate_weight, up_weight, down_weight
):
    groups = lax.axis_size("expert")
    n_dp = lax.axis_size("dp")
    chips = n_dp // 2
    experts_all, unit_piece, piece_width = gate_weight.shape
    units_all = unit_piece * groups
    row_count = rows_in.shape[0]
    half = row_count // 2
    share = half // chips
    tail = 3 * unit_piece - LANES
    per = LANES // tail
    core = lax.axis_index("dp") % 2
    partners = [(i, i ^ 1) for i in range(n_dp)]
    same_core = [[2 * i + c for i in range(chips)] for c in range(2)]

    def among_chips(blocks):
        return lax.all_to_all(
            blocks, "dp", split_axis=0, concat_axis=0, tiled=True, axis_index_groups=same_core
        )

    in_vmem = pl.BlockSpec(memory_space=pltpu.VMEM)
    in_smem = pl.BlockSpec(memory_space=pltpu.SMEM)
    in_place = pl.BlockSpec(memory_space=pl.ANY)
    roomy = pltpu.CompilerParams(vmem_limit_bytes=VMEM_LIMIT)
    core_index = core.reshape(1).astype(jnp.int32)

    outgoing = pl.pallas_call(
        functools.partial(gather_kernel, unit_piece),
        in_specs=[in_smem, in_place, in_place, in_place],
        out_specs=in_place,
        out_shape=jax.ShapeDtypeStruct((groups, 3 * unit_piece, piece_width), jnp.bfloat16),
        scratch_shapes=[
            pltpu.VMEM((3, *gate_weight.shape), jnp.bfloat16),
            pltpu.VMEM((3, groups, unit_piece, piece_width), jnp.bfloat16),
            pltpu.SemaphoreType.DMA((3,)),
            pltpu.SemaphoreType.DMA((3,)),
        ],
        compiler_params=pltpu.CompilerParams(vmem_limit_bytes=GATHER_VMEM_LIMIT),
    )(expert_of_group, gate_weight, up_weight, down_weight)
    fetched = lax.all_to_all(outgoing, "expert", split_axis=0, concat_axis=0, tiled=True)

    position = jnp.arange(row_count, dtype=jnp.int32)
    live_mask = (position < live_rows[0]).astype(jnp.float32)
    scaled = (out_grad.astype(jnp.float32) * (route_weight * live_mask)[:, None]).astype(
        jnp.bfloat16
    )
    both = jnp.concatenate([rows_in, scaled], axis=1)
    both, fetched = lax.optimization_barrier((both, fetched))
    rows_all = lax.all_gather(both, "expert", axis=0, tiled=True)

    product_flops = 2 * half * 3 * units_all * piece_width
    product_bytes = 2 * (half + groups * piece_width) * 3 * unit_piece * 16
    sent = pl.pallas_call(
        functools.partial(sent_kernel, unit_piece),
        in_specs=[in_smem, in_vmem, in_vmem, in_vmem],
        out_specs=in_vmem,
        out_shape=jax.ShapeDtypeStruct((half, 3 * units_all), jnp.bfloat16),
        compiler_params=roomy,
        cost_estimate=pl.CostEstimate(
            flops=product_flops, bytes_accessed=product_bytes, transcendentals=0
        ),
    )(core_index, rows_in, scaled, fetched)
    got = lax.ppermute(sent, "dp", partners)
    paired = pl.pallas_call(
        functools.partial(paired_kernel, unit_piece),
        in_specs=[in_smem, in_vmem, in_vmem, in_vmem, in_vmem],
        out_specs=in_vmem,
        out_shape=jax.ShapeDtypeStruct((half, 3 * units_all), jnp.bfloat16),
        compiler_params=roomy,
        cost_estimate=pl.CostEstimate(
            flops=product_flops, bytes_accessed=product_bytes, transcendentals=0
        ),
    )(core_index, rows_in, scaled, fetched, got).reshape(chips, share, 3 * units_all)
    parts = among_chips(paired)
    grad_blocks = 2 * units_all // LANES
    pieces, grads = pl.pallas_call(
        functools.partial(hidden_kernel, groups, unit_piece),
        out_shape=(
            jax.ShapeDtypeStruct((groups, share // 2, 3 * LANES), jnp.bfloat16),
            jax.ShapeDtypeStruct((grad_blocks, share, LANES), jnp.bfloat16),
        ),
        compiler_params=roomy,
    )(parts)

    pieces = lax.all_to_all(pieces, "expert", split_axis=0, concat_axis=0, tiled=True)
    packed_count = groups + groups // per
    copies = pl.pallas_call(
        functools.partial(pack_kernel, groups, tail),
        out_shape=jax.ShapeDtypeStruct(
            (chips, packed_count + grad_blocks, share, LANES), jnp.bfloat16
        ),
        compiler_params=roomy,
    )(pieces, grads)
    hidden_mine = among_chips(copies)
    hidden_other = lax.ppermute(hidden_mine, "dp", partners)

    def turned(hidden, *first):
        return pl.pallas_call(
            functools.partial(turned_kernel, tail, unit_piece),
            in_specs=[in_smem] + [in_vmem] * (2 + len(first)),
            out_specs=(in_vmem, in_vmem),
            out_shape=(
                jax.ShapeDtypeStruct((groups, 3 * unit_piece, half), jnp.bfloat16),
                jax.ShapeDtypeStruct((half * (1 + len(first)), piece_width), jnp.bfloat16),
            ),
            compiler_params=pltpu.CompilerParams(vmem_limit_bytes=TURNED_VMEM_LIMIT),
            cost_estimate=pl.CostEstimate(
                flops=2 * row_count * units_all * piece_width,
                bytes_accessed=7 * 1024 * 1024,
                transcendentals=0,
            ),
        )(core_index, hidden, fetched, *first)

    turned_mine, grad_mine = turned(hidden_mine)
    turned_other, rows_grad = turned(hidden_other, grad_mine)

    rows_by_half = rows_all.reshape(groups, 2, half, 2 * piece_width)
    grad_shape = (experts_all, unit_piece, piece_width)
    gate_grad, up_grad, down_grad = pl.pallas_call(
        functools.partial(weight_kernel, unit_piece, 8),
        in_specs=[in_smem, in_smem, in_place, in_place, in_place],
        out_specs=(in_vmem,) * 3,
        out_shape=tuple(jax.ShapeDtypeStruct(grad_shape, jnp.bfloat16) for _ in range(3)),
        scratch_shapes=[
            pltpu.VMEM((groups, 3 * unit_piece, row_count), jnp.bfloat16),
            pltpu.VMEM((groups, row_count, 2 * piece_width), jnp.bfloat16),
            pltpu.VMEM((experts_all, 3 * unit_piece, piece_width), jnp.float32),
            pltpu.SemaphoreType.DMA((4 * 8,)),
        ],
        compiler_params=pltpu.CompilerParams(vmem_limit_bytes=LARGE_VMEM_LIMIT),
        cost_estimate=pl.CostEstimate(
            flops=4 * groups * row_count * LANES * 3 * LANES,
            bytes_accessed=12 * 1024 * 1024,
            transcendentals=0,
        ),
    )(expert_of_group, core_index, turned_mine, turned_other, rows_by_half)

    return (rows_grad, gate_grad, up_grad, down_grad)


def solution(mesh):
    return jax.shard_map(
        shards,
        mesh=mesh,
        in_specs=(
            P("expert", "dp"),
            P("expert", "dp"),
            P("expert"),
            P("expert"),
            P(),
            P(None, "expert", "dp"),
            P(None, "expert", "dp"),
            P(None, "expert", "dp"),
        ),
        out_specs=(
            P("expert", "dp"),
            P(None, "expert", "dp"),
            P(None, "expert", "dp"),
            P(None, "expert", "dp"),
        ),
        check_vma=False,
    )
```
